512 devices in a mesh: head: 8 (over y), seq: 64 (over z, x, core).
Axes of the slice: x: 4, y: 8, z: 8, core: 2. Of those that a mesh axis runs over, the one named last changes fastest.
Arguments:
- q_in: bfloat16 [16384, 3072], P('seq', 'head'), may hold values from -32 to 32
- k_in: bfloat16 [16384, 3072], P('seq', 'head'), may hold values from -32 to 32
- v_in: bfloat16 [16384, 3072], P('seq', 'head'), may hold values from -6 to 6
- q_rank: int32 [2, 24, 16384], P(None, 'head', 'seq'), may hold values from 0 to 16383, as said below
- k_rank: int32 [2, 24, 16384], P(None, 'head', 'seq'), may hold values from 0 to 16383, as said below
- w_out: bfloat16 [3072, 3072], P(None, 'head'), may hold values from -0.109375 to 0.109375
Outputs:
- mixed: bfloat16 [16384, 3072], P('seq', 'head')
The draws below stay inside these ranges and needn't reach their ends.
Inputs may be any that keep to these rules, and one draw needn't show every extreme that they name: Each row q_rank[r, h, :] is a permutation of the 16384 positions; for every round, head and pair of seq shards s and d, at most 8 tokens of shard s have positions from d * 256 to (d + 1) * 256 - 1, and for every round, head and seq shard s, some shard d receives exactly 8 tokens of s. `k_rank`: as for q_rank, independently drawn.
All inputs are finite; a program needn't handle non-finite values.
Results may differ from the reference program's by a relative error of at most 0.0064.
Values may be sent and summed in bfloat16 or wider, within the bound.
A program may use at most 64 MiB of HBM per device.

```python
import math
import jax
import jax.numpy as jnp
from jax import lax

D = 3072
HEADS = 24
HD = 128
CLUSTER = 256
ROUNDS = 2
TOK_DEV = 256
TOKENS = 16384
CAP = 8


def position_law(key_base):
    unit_size = CAP // 2
    shard_count = TOK_DEV // unit_size
    key_a, key_b, key_c, key_d = jax.random.split(key_base, 4)
    relabel = jax.random.permutation(key_a, shard_count).astype(jnp.int32)
    relabel_inv = jnp.argsort(relabel).astype(jnp.int32)
    offset_order = jax.random.permutation(key_b, shard_count).astype(jnp.int32)
    offsets = jnp.concatenate([offset_order[:1], offset_order[:shard_count - 1]])
    local_perm = jax.vmap(lambda sub: jax.random.permutation(sub, TOK_DEV))(jax.random.split(key_c, shard_count)).astype(jnp.int32)
    range_perm = jax.vmap(lambda sub: jax.random.permutation(sub, TOK_DEV))(jax.random.split(key_d, shard_count)).astype(jnp.int32)
    unit_index = local_perm // unit_size
    within = local_perm % unit_size
    source = jnp.arange(shard_count, dtype=jnp.int32)[:, None]
    target = relabel[(relabel_inv[source] + offsets[unit_index]) % shard_count]
    local_pos = range_perm[target, unit_index * unit_size + within]
    return (target * TOK_DEV + local_pos).reshape(TOKENS).astype(jnp.int32)


def draw_q_rank(key, part):
    key = jax.random.fold_in(key, 11)
    keys_all = jax.random.split(key, ROUNDS * HEADS)
    return jax.vmap(position_law)(keys_all).reshape(ROUNDS, HEADS, TOKENS).astype(jnp.int32)


def draw_k_rank(key, part):
    key = jax.random.fold_in(key, 23)
    keys_all = jax.random.split(key, ROUNDS * HEADS)
    return jax.vmap(position_law)(keys_all).reshape(ROUNDS, HEADS, TOKENS).astype(jnp.int32)


def feature_law(key_base, top_scale):
    key_a, key_b = jax.random.split(key_base)
    values = jnp.clip(jax.random.normal(key_a, (TOKENS, HEADS * HD), jnp.float32), -4.0, 4.0)
    scales = jnp.exp(jax.random.uniform(key_b, (TOKENS, 1), jnp.float32, 0.0, math.log(top_scale)))
    return values * scales


def draw_q_in(key, part):
    key = jax.random.fold_in(key, 3)
    values = feature_law(key, 1.5)
    return values.astype(jnp.bfloat16)


def draw_k_in(key, part):
    key = jax.random.fold_in(key, 5)
    values = feature_law(key, 1.5)
    return values.astype(jnp.bfloat16)


def shard_levels(key, extent, cuts, low, high):
    def one(axis_at, blocks):
        draws = jax.random.uniform(jax.random.fold_in(jax.random.fold_in(key, 6), axis_at), (blocks,), jnp.float32, low / len(cuts), high / len(cuts))
        return jnp.repeat(jnp.exp(draws), extent[axis_at] // blocks).reshape((-1,) + (1,) * (len(extent) - axis_at - 1))

    loudness = one(*cuts[0])
    for cut in cuts[1:]:
        loudness = loudness * one(*cut)
    return loudness


def noise(rng, dims, spread, reach, cuts=(), kind=jnp.bfloat16):
    array = jax.random.normal(rng, dims, jnp.float32) * spread
    if len(cuts) > 0:
        array = shard_levels(rng, dims, cuts, -0.22, 0.18) * array
    return jnp.clip(array, min=-reach, max=reach).astype(kind)


def setup_inputs(seed: int = 0) -> dict:
    arg_keys = jax.random.split(jax.random.key(seed), 7)
    return {
        "q_in": draw_q_in(jax.random.fold_in(arg_keys[6], 71), 0),
        "k_in": draw_k_in(jax.random.fold_in(arg_keys[6], 71), 0),
        "v_in": noise(arg_keys[2], (TOKENS, HEADS * HD), 1.0, 6.0, ((0, 64), (1, 8))),
        "q_rank": draw_q_rank(jax.random.fold_in(arg_keys[6], 71), 0),
        "k_rank": draw_k_rank(jax.random.fold_in(arg_keys[6], 71), 0),
        "w_out": noise(arg_keys[5], (HEADS * HD, D), (HEADS * HD) ** -0.5, 0.109375, ((1, 8),)),
    }


def attend_head(q_head, k_head, v_head, q_order, k_order):
    q_sorted = jnp.zeros_like(q_head).at[q_order].set(q_head)
    k_sorted = jnp.zeros_like(k_head).at[k_order].set(k_head)
    v_sorted = jnp.zeros_like(v_head).at[k_order].set(v_head)
    groups = TOKENS // CLUSTER
    q_blocks = q_sorted.reshape(groups, CLUSTER, HD).astype(jnp.float32)
    k_blocks = k_sorted.reshape(groups, CLUSTER, HD).astype(jnp.float32)
    v_blocks = v_sorted.reshape(groups, CLUSTER, HD).astype(jnp.float32)
    scores = jnp.einsum("cqe,cke->cqk", q_blocks, k_blocks) * (HD ** -0.5)
    peak_score = jnp.max(scores, axis=2, keepdims=True)
    row_total = jnp.sum(jnp.exp(scores - peak_score), axis=2, keepdims=True)
    log_total = peak_score + jnp.log(row_total)
    weights = jnp.exp(scores - log_total).astype(jnp.bfloat16)
    result = jnp.einsum("cqk,cke->cqe", weights.astype(jnp.float32), v_blocks).astype(jnp.bfloat16)
    result = result.reshape(TOKENS, HD)[q_order]
    log_rows = log_total.reshape(TOKENS)[q_order]
    return result, log_rows


def reference(q_in, k_in, v_in, q_rank, k_rank, w_out):
    q_heads = jnp.transpose(q_in.reshape(TOKENS, HEADS, HD), (1, 0, 2))
    k_heads = jnp.transpose(k_in.reshape(TOKENS, HEADS, HD), (1, 0, 2))
    v_heads = jnp.transpose(v_in.reshape(TOKENS, HEADS, HD), (1, 0, 2))
    out_rows = []
    out_logs = []
    for round_idx in range(ROUNDS):
        result, log_rows = lax.map(lambda items: attend_head(*items), (q_heads, k_heads, v_heads, q_rank[round_idx], k_rank[round_idx]))
        out_rows.append(result)
        out_logs.append(log_rows)
    stacked_rows = jnp.stack(out_rows)
    stacked_logs = jnp.stack(out_logs)
    peak_log = jnp.max(stacked_logs, axis=0, keepdims=True)
    round_share = jnp.exp(stacked_logs - peak_log)
    round_mix = round_share / jnp.sum(round_share, axis=0, keepdims=True)
    attended = jnp.sum(round_mix[..., None] * stacked_rows.astype(jnp.float32), axis=0)
    attended = jnp.transpose(attended, (1, 0, 2)).reshape(TOKENS, HEADS * HD).astype(jnp.bfloat16)
    return jnp.dot(attended, w_out, preferred_element_type=jnp.float32).astype(jnp.bfloat16)
```

```python
import functools

import jax
import jax.numpy as jnp
from jax import lax
from jax.experimental import pallas as pl
from jax.experimental.pallas import tpu as pltpu
from jax.sharding import PartitionSpec as P

MESH = pl.DeviceIdType.MESH
HD = 128
EMPTY = 64.0
F32 = jnp.float32
BF16 = jnp.bfloat16


def dot(a, b, dims=((1,), (0,)), precision=None):
    return lax.dot_general(a, b, (dims, ((), ())), preferred_element_type=F32, precision=precision)


def kernel(
    sizes, q_ref, k_ref, v_ref, qrank_ref, krank_ref, w_hbm, out_ref,
    w_ref, send_x, recv_x, send_o, recv_o, send_l, recv_l, gath, pq_ref, tq_ref, oq_ref,
    w_sem, sx_sem, rx_sem, so_sem, ro_sem, sl_sem, rl_sem, sg_sem, rg_sem,
):
    nseq, nhead, per, rounds, length = sizes
    cap = 2 * length // nseq
    slots = nseq * cap
    me = lax.axis_index("seq")
    my_head = lax.axis_index("head")
    barrier = pltpu.get_barrier_semaphore()

    def peer_of(step):
        outer = 8 if nseq % 8 == 0 else 1
        inner = nseq // outer
        hop, rest = step % outer, step // outer
        return ((me // inner + hop) % outer) * inner + (me % inner + rest) % inner

    @pl.loop(1, nseq)
    def _(step):
        pl.semaphore_signal(barrier, inc=1, device_id={"seq": peer_of(step)}, device_id_type=MESH)

    @pl.loop(1, nhead)
    def _(step):
        pl.semaphore_signal(barrier, inc=1, device_id={"head": (my_head + step) % nhead}, device_id_type=MESH)

    w_copy = pltpu.make_async_copy(w_hbm, w_ref, w_sem)
    w_copy.start()

    shard_ids = lax.broadcasted_iota(jnp.int32, (nseq, length), 0)
    slot_ids = lax.broadcasted_iota(jnp.int32, (slots, length), 0)
    earlier = (
        lax.broadcasted_iota(jnp.int32, (length, length), 0) < lax.broadcasted_iota(jnp.int32, (length, length), 1)
    ).astype(F32).astype(BF16)

    def route(rank_row):
        target = rank_row // length
        owner = (target == shard_ids).astype(F32)
        before = dot(owner.astype(BF16), earlier)
        ordinal = jnp.sum(owner * before, axis=0, keepdims=True)
        slot = target * cap + ordinal.astype(jnp.int32)
        place = (slot_ids == slot).astype(F32).astype(BF16)
        return owner, ordinal, place, jnp.sum(owner, axis=1, keepdims=True)

    def by_peer(rows):
        return rows.reshape(nseq, cap, HD)

    def pack(h):
        cols = slice(h * HD, (h + 1) * HD)
        q_rows, k_rows, v_rows = [], [], []
        for r in range(rounds):
            owner, ordinal, place, _ = route(qrank_ref[r, h : h + 1, :])
            pq_ref[r, h] = place
            tq_ref[r, h] = owner
            oq_ref[r, h] = ordinal
            q_rows.append(by_peer(dot(place, q_ref[:, cols])))
            _, _, place, count = route(krank_ref[r, h : h + 1, :])
            both = dot(place, jnp.concatenate([k_ref[:, cols], v_ref[:, cols]], axis=1))
            seat = lax.broadcasted_iota(jnp.int32, (nseq, cap, HD), 1).astype(F32)
            filled = seat < jnp.broadcast_to(count, (nseq, HD))[:, None, :]
            k_rows.append(jnp.where(filled, by_peer(both[:, :HD]), EMPTY))
            v_rows.append(by_peer(both[:, HD:]))
        for i, rows in enumerate((q_rows, k_rows, v_rows)):
            send_x[h, :, i] = jnp.concatenate(rows, axis=1).astype(BF16)

    def push(send, recv, send_sem, recv_sem, h):
        recv[h, me] = send[h, me]

        @pl.loop(1, nseq)
        def _(step):
            peer = peer_of(step)
            pltpu.make_async_remote_copy(
                src_ref=send.at[h, peer],
                dst_ref=recv.at[h, me],
                send_sem=send_sem.at[h],
                recv_sem=recv_sem.at[h],
                device_id={"seq": peer},
                device_id_type=MESH,
            ).start()

    def await_all(buf, sem, h):
        part = buf.at[h, pl.ds(0, nseq - 1)]
        pltpu.make_async_copy(part, part, sem.at[h]).wait()

    def attend(h):
        lane = lax.broadcasted_iota(jnp.int32, (slots, HD), 1)
        row = lax.broadcasted_iota(jnp.int32, (slots, HD), 0)
        column_shard = lax.broadcasted_iota(jnp.int32, (nseq, slots), 1) // cap
        same_shard = column_shard == lax.broadcasted_iota(jnp.int32, (nseq, slots), 0)
        block = slots // 2
        out_rows = []
        logs = jnp.zeros((nseq, HD), F32)
        for r in range(rounds):

            def half(i):
                tile = recv_x[h, :, i].astype(F32)
                return tile[:, r * cap : (r + 1) * cap].reshape(slots, HD)

            q_all = half(0).astype(BF16)
            k_all = half(1)
            empty = k_all > 0.5 * EMPTY
            k_all = k_all.astype(BF16)
            v_all = half(2).astype(BF16)
            empty = jnp.concatenate([empty.astype(F32)] * (block // HD), axis=1) > 0.5 if block > HD else empty[:, :block]
            parts, log_parts = [], []
            for c in range(2):
                scores = dot(k_all, q_all[c * block : (c + 1) * block], ((1,), (1,))) * HD ** (-0.5)
                scores = jnp.where(empty, -1e30, scores)
                peak = jnp.max(scores, axis=0, keepdims=True)
                weights = jnp.exp(scores - peak)
                total = jnp.sum(weights, axis=0, keepdims=True)
                weights = (weights * (1.0 / total)).astype(BF16)
                parts.append(dot(v_all, weights, ((0,), (0,))).T)
                log_parts.append(peak + jnp.log(total))
            out_rows.append(by_peer(jnp.concatenate(parts, axis=0)))
            log_row = jnp.concatenate(log_parts, axis=1)
            spread = jnp.where(same_shard, log_row, 0.0)
            seat = (lane == row % cap + r * cap).astype(F32)
            logs = logs + dot(spread, seat, precision=lax.Precision.HIGHEST)
        send_o[h] = jnp.concatenate(out_rows, axis=1).astype(BF16)
        for d in range(nseq):
            send_l[h, d] = logs[d : d + 1]

    def mix(h):
        logs_in = jnp.concatenate([recv_l[h, d] for d in range(nseq)], axis=0)
        seat = lax.broadcasted_iota(jnp.int32, (cap, length), 0).astype(F32)
        logs, rows = [], []
        tile = recv_o[h].astype(F32)
        for r in range(rounds):
            of_owner = dot(logs_in, tq_ref[r, h], ((0,), (0,)), precision=lax.Precision.HIGHEST)
            mine = jnp.where(seat == oq_ref[r, h], of_owner[r * cap : (r + 1) * cap], 0.0)
            logs.append(jnp.sum(mine, axis=0, keepdims=True))
            part = tile[:, r * cap : (r + 1) * cap].reshape(slots, HD).astype(BF16)
            rows.append(dot(part, pq_ref[r, h], ((0,), (0,))))
        peak = functools.reduce(jnp.maximum, logs)
        shares = [jnp.exp(log - peak) for log in logs]
        total = functools.reduce(jnp.add, shares)
        mixed = functools.reduce(jnp.add, [share / total * row for share, row in zip(shares, rows)])
        gath[h, my_head] = mixed.T.astype(BF16)

    def push_heads(h):
        @pl.loop(1, nhead)
        def _(step):
            pltpu.make_async_remote_copy(
                src_ref=gath.at[h, my_head],
                dst_ref=gath.at[h, my_head],
                send_sem=sg_sem.at[h],
                recv_sem=rg_sem.at[h],
                device_id={"head": (my_head + step) % nhead},
                device_id_type=MESH,
            ).start()

    def await_heads(sem, h):
        part = gath.at[h, pl.ds(0, nhead - 1)]
        pltpu.make_async_copy(part, part, sem.at[h]).wait()

    for h in range(per):
        pack(h)
        if h == 0:
            pl.semaphore_wait(barrier, nseq + nhead - 2)
        push(send_x, recv_x, sx_sem, rx_sem, h)
    for h in range(per):
        await_all(recv_x, rx_sem, h)
        attend(h)
        push(send_o, recv_o, so_sem, ro_sem, h)
        push(send_l, recv_l, sl_sem, rl_sem, h)
    for h in range(per):
        await_all(recv_o, ro_sem, h)
        await_all(recv_l, rl_sem, h)
        mix(h)
        push_heads(h)
    w_copy.wait()
    total = None
    for h in range(per):
        await_heads(rg_sem, h)
        left = jnp.concatenate([gath[h, y] for y in range(nhead)], axis=1)
        right = jnp.concatenate([w_ref[(y * per + h) * HD : (y * per + h + 1) * HD] for y in range(nhead)], axis=0)
        part = dot(left, right)
        total = part if total is None else total + part
    out_ref[...] = total.astype(BF16)
    for h in range(per):
        await_all(send_x, sx_sem, h)
        await_all(send_o, so_sem, h)
        await_all(send_l, sl_sem, h)
        await_heads(sg_sem, h)


def solution(mesh):
    nseq, nhead = mesh.shape["seq"], mesh.shape["head"]

    def body(q_in, k_in, v_in, q_rank, k_rank, w_out):
        length, width = q_in.shape
        rounds, per, _ = q_rank.shape
        cap = 2 * length // nseq
        slots = nseq * cap
        vmem = pl.BlockSpec(memory_space=pltpu.VMEM)
        scratch = [
            pltpu.VMEM(w_out.shape, BF16),
            pltpu.VMEM((per, nseq, 3, rounds * cap, HD), BF16),
            pltpu.VMEM((per, nseq, 3, rounds * cap, HD), BF16),
            pltpu.VMEM((per, nseq, rounds * cap, HD), BF16),
            pltpu.VMEM((per, nseq, rounds * cap, HD), BF16),
            pltpu.VMEM((per, nseq, 1, HD), F32),
            pltpu.VMEM((per, nseq, 1, HD), F32),
            pltpu.VMEM((per, nhead, length, HD), BF16),
            pltpu.VMEM((rounds, per, slots, length), BF16),
            pltpu.VMEM((rounds, per, nseq, length), F32),
            pltpu.VMEM((rounds, per, 1, length), F32),
            pltpu.SemaphoreType.DMA,
        ] + [pltpu.SemaphoreType.DMA((per,))] * 8
        return pl.pallas_call(
            functools.partial(kernel, (nseq, nhead, per, rounds, length)),
            out_shape=jax.ShapeDtypeStruct((length, w_out.shape[1]), BF16),
            in_specs=[vmem] * 5 + [pl.BlockSpec(memory_space=pl.ANY)],
            out_specs=vmem,
            scratch_shapes=scratch,
            compiler_params=pltpu.CompilerParams(
                collective_id=0, has_side_effects=True, vmem_limit_bytes=48 * 1024 * 1024
            ),
        )(q_in, k_in, v_in, q_rank, k_rank, w_out)

    return jax.shard_map(
        body,
        mesh=mesh,
        in_specs=(
            P("seq", "head"),
            P("seq", "head"),
            P("seq", "head"),
            P(None, "head", "seq"),
            P(None, "head", "seq"),
            P(None, "head"),
        ),
        out_specs=P("seq", "head"),
        check_vma=False,
    )
```

```python
import functools

import jax
import jax.numpy as jnp
from jax import lax
from jax.experimental import pallas as pl
from jax.experimental.pallas import tpu as pltpu
from jax.sharding import PartitionSpec as P

MESH = pl.DeviceIdType.MESH
HD = 128
PLANES = 8
EMPTY = 64.0
F32 = jnp.float32
BF16 = jnp.bfloat16


def dot(a, b, dims=((1,), (0,)), precision=None):
    return lax.dot_general(a, b, (dims, ((), ())), preferred_element_type=F32, precision=precision)


def kernel(
    sizes, q_hbm, k_hbm, v_hbm, qrank_ref, krank_ref, w_hbm, out_ref,
    w_ref, shard, seats, packed, recv_x, send_o, recv_o, send_l, recv_l, gath, tq_ref, oq_ref,
    w_sem, seat_send, seat_recv, ring_send, ring_recv,
    sx_sem, rx_sem, so_sem, ro_sem, sl_sem, rl_sem, sg_sem, rg_sem,
):
    nseq, nhead, per, rounds, length = sizes
    cap = 2 * length // nseq
    slots = nseq * cap
    inner = nseq // PLANES
    me = lax.axis_index("seq")
    my_head = lax.axis_index("head")
    my_plane, my_place = me // inner, me % inner
    barrier = pltpu.get_barrier_semaphore()

    def plane_at(hop):
        return (my_plane + hop + PLANES) % PLANES

    def peer_of(step):
        return plane_at(step % PLANES) * inner + (my_place + step // PLANES) % inner

    @pl.loop(1, nseq)
    def _(step):
        pl.semaphore_signal(barrier, inc=1, device_id={"seq": peer_of(step)}, device_id_type=MESH)

    @pl.loop(1, nhead)
    def _(step):
        pl.semaphore_signal(barrier, inc=1, device_id={"head": (my_head + step) % nhead}, device_id_type=MESH)

    for h in range(per):
        for i, source in enumerate((q_hbm, k_hbm, v_hbm)):
            pltpu.make_async_copy(source.at[:, pl.ds(h * HD, HD)], shard.at[h, 0, i], ring_recv.at[h, 0]).start()
    w_copy = pltpu.make_async_copy(w_hbm, w_ref, w_sem)
    w_copy.start()

    def find_seats():
        shard_ids = lax.broadcasted_iota(jnp.int32, (nseq, length), 0)
        earlier = (
            lax.broadcasted_iota(jnp.int32, (length, length), 0)
            < lax.broadcasted_iota(jnp.int32, (length, length), 1)
        ).astype(F32).astype(BF16)
        seats[0] = jnp.zeros(seats.shape[1:], F32)
        for side, rank_ref in enumerate((qrank_ref, krank_ref)):
            for r in range(rounds):
                for h in range(per):
                    target = rank_ref[r, h : h + 1, :] // length
                    owner = (target == shard_ids).astype(F32)
                    before = dot(owner.astype(BF16), earlier)
                    ordinal = jnp.sum(owner * before, axis=0, keepdims=True)
                    row = (side * rounds + r) * per + h
                    seats[0, row : row + 1] = (target * cap).astype(F32) + ordinal
                    if side == 0:
                        tq_ref[r, h] = owner
                        oq_ref[r, h] = ordinal

    def seat_row(j, side, r, h):
        row = (side * rounds + r) * per + h
        return seats[j, row : row + 1].astype(jnp.int32)

    def ring(buf, h, send_sem, recv_sem, source, target, hop):
        at = (lambda j: buf.at[j]) if h is None else (lambda j: buf.at[h, j])
        pltpu.make_async_remote_copy(
            src_ref=at(source),
            dst_ref=at(target),
            send_sem=send_sem,
            recv_sem=recv_sem.at[target] if h is None else recv_sem.at[h, target],
            device_id={"seq": plane_at(hop) * inner + my_place},
            device_id_type=MESH,
        ).start()

    def ring_shards(h, stage):
        for (source, target), hop in zip(((0, 1), (0, 2)) if stage == 0 else ((1, 3), (2, 4)), (1, -1)):
            ring(shard, h, ring_send.at[h], ring_recv, source, target, hop)

    def ring_seats(stage):
        for (source, target), hop in zip(((0, 1), (0, 2)) if stage == 0 else ((1, 3), (2, 4)), (1, -1)):
            ring(seats, None, seat_send, seat_recv, source, target, hop)

    def await_shard(h, j):
        pltpu.make_async_copy(shard.at[h, j], shard.at[h, j], ring_recv.at[h, j]).wait()

    def await_seats(j):
        pltpu.make_async_copy(seats.at[j], seats.at[j], seat_recv.at[j]).wait()

    def pack(h, j, targets):
        n = len(targets) * inner
        ids = [lax.broadcasted_iota(jnp.int32, (inner * cap, length), 0) + plane * (inner * cap) for plane, _ in targets]
        ids = jnp.concatenate(ids, axis=0)
        q_all = shard[h, j, 0]
        kv_all = jnp.concatenate([shard[h, j, 1], shard[h, j, 2]], axis=1)
        q_rows, k_rows, v_rows = [], [], []
        for r in range(rounds):
            place = (ids == seat_row(j, 0, r, h)).astype(F32).astype(BF16)
            q_rows.append(dot(place, q_all).reshape(n, cap, HD))
            place = (ids == seat_row(j, 1, r, h)).astype(F32)
            filled = jnp.sum(place, axis=1, keepdims=True) > 0.5
            both = dot(place.astype(BF16), kv_all)
            k_rows.append(jnp.where(filled, both[:, :HD], EMPTY).reshape(n, cap, HD))
            v_rows.append(both[:, HD:].reshape(n, cap, HD))
        for i, rows in enumerate((q_rows, k_rows, v_rows)):
            rows = jnp.concatenate(rows, axis=1).astype(BF16)
            for t, (_, index) in enumerate(targets):
                packed[h, index, :, i] = rows[t * inner : (t + 1) * inner]

    def deliver(h, index, place, plane, source):
        pltpu.make_async_remote_copy(
            src_ref=packed.at[h, index, place],
            dst_ref=recv_x.at[h, source],
            send_sem=sx_sem.at[h],
            recv_sem=rx_sem.at[h],
            device_id={"seq": plane * inner + place},
            device_id_type=MESH,
        ).start()

    def near(h, js):
        for j in js:
            source = plane_at((0, -1, 1, -2, 2)[j]) * inner + my_place
            pack(h, j, [(my_plane, j)])
            recv_x[h, source] = packed[h, j, my_place]

            @pl.loop(1, inner)
            def _(step):
                deliver(h, j, (my_place + step) % inner, my_plane, source)

    def relay(h):
        for j, way in ((3, 1), (4, -1)):
            source = plane_at(-2 * way) * inner + my_place
            one, two = 2 * j - 1, 2 * j
            pack(h, j, [(my_plane, j), (plane_at(way), one), (plane_at(2 * way), two)])

            @pl.loop(0, inner)
            def _(step):
                deliver(h, one, (my_place + step) % inner, plane_at(way), source)

            odd = j - 3
            half = (inner + 1 - odd) // 2

            @pl.loop(0, half)
            def _(step):
                deliver(h, two, 2 * ((my_place // 2 + step) % half) + odd, plane_at(2 * way), source)

            recv_x[h, source] = packed[h, j, my_place]

            @pl.loop(1, inner)
            def _(step):
                deliver(h, j, (my_place + step) % inner, my_plane, source)

    def await_rows(buf, sem, h):
        part = recv_x.at[h, pl.ds(0, nseq - 5)]
        pltpu.make_async_copy(part, part, sem.at[h]).wait()

    def by_peer(rows):
        return rows.reshape(nseq, cap, HD)

    def push(send, recv, send_sem, recv_sem, h):
        recv[h, me] = send[h, me]

        @pl.loop(1, nseq)
        def _(step):
            peer = peer_of(step)
            pltpu.make_async_remote_copy(
                src_ref=send.at[h, peer],
                dst_ref=recv.at[h, me],
                send_sem=send_sem.at[h],
                recv_sem=recv_sem.at[h],
                device_id={"seq": peer},
                device_id_type=MESH,
            ).start()

    def await_all(buf, sem, h):
        part = buf.at[h, pl.ds(0, nseq - 1)]
        pltpu.make_async_copy(part, part, sem.at[h]).wait()

    def attend(h):
        lane = lax.broadcasted_iota(jnp.int32, (slots, HD), 1)
        row = lax.broadcasted_iota(jnp.int32, (slots, HD), 0)
        column_shard = lax.broadcasted_iota(jnp.int32, (nseq, slots), 1) // cap
        same_shard = column_shard == lax.broadcasted_iota(jnp.int32, (nseq, slots), 0)
        block = slots // 2
        out_rows = []
        logs = jnp.zeros((nseq, HD), F32)
        for r in range(rounds):

            def half(i):
                tile = recv_x[h, :, i].astype(F32)
                return tile[:, r * cap : (r + 1) * cap].reshape(slots, HD)

            q_all = half(0).astype(BF16)
            k_all = half(1)
            empty = k_all > 0.5 * EMPTY
            k_all = k_all.astype(BF16)
            v_all = half(2).astype(BF16)
            empty = jnp.concatenate([empty.astype(F32)] * (block // HD), axis=1) > 0.5 if block > HD else empty[:, :block]
            parts, log_parts = [], []
            for c in range(2):
                scores = dot(k_all, q_all[c * block : (c + 1) * block], ((1,), (1,))) * HD ** (-0.5)
                scores = jnp.where(empty, -1e30, scores)
                peak = jnp.max(scores, axis=0, keepdims=True)
                weights = jnp.exp(scores - peak)
                total = jnp.sum(weights, axis=0, keepdims=True)
                weights = (weights * (1.0 / total)).astype(BF16)
                parts.append(dot(v_all, weights, ((0,), (0,))).T)
                log_parts.append(peak + jnp.log(total))
            out_rows.append(by_peer(jnp.concatenate(parts, axis=0)))
            log_row = jnp.concatenate(log_parts, axis=1)
            spread = jnp.where(same_shard, log_row, 0.0)
            seat = (lane == row % cap + r * cap).astype(F32)
            logs = logs + dot(spread, seat, precision=lax.Precision.HIGHEST)
        send_o[h] = jnp.concatenate(out_rows, axis=1).astype(BF16)
        for d in range(nseq):
            send_l[h, d] = logs[d : d + 1]

    def mix(h):
        logs_in = jnp.concatenate([recv_l[h, d] for d in range(nseq)], axis=0)
        seat = lax.broadcasted_iota(jnp.int32, (cap, length), 0).astype(F32)
        logs, rows = [], []
        tile = recv_o[h].astype(F32)
        slot_ids = lax.broadcasted_iota(jnp.int32, (slots, length), 0)
        for r in range(rounds):
            of_owner = dot(logs_in, tq_ref[r, h], ((0,), (0,)), precision=lax.Precision.HIGHEST)
            mine = jnp.where(seat == oq_ref[r, h], of_owner[r * cap : (r + 1) * cap], 0.0)
            logs.append(jnp.sum(mine, axis=0, keepdims=True))
            part = tile[:, r * cap : (r + 1) * cap].reshape(slots, HD).astype(BF16)
            place = (slot_ids == seat_row(0, 0, r, h)).astype(F32).astype(BF16)
            rows.append(dot(part, place, ((0,), (0,))))
        peak = functools.reduce(jnp.maximum, logs)
        shares = [jnp.exp(log - peak) for log in logs]
        total = functools.reduce(jnp.add, shares)
        mixed = functools.reduce(jnp.add, [share / total * row for share, row in zip(shares, rows)])
        gath[h, my_head] = mixed.T.astype(BF16)

    def push_heads(h):
        if nhead == 1:
            return
        @pl.loop(1, nhead)
        def _(step):
            pltpu.make_async_remote_copy(
                src_ref=gath.at[h, my_head],
                dst_ref=gath.at[h, my_head],
                send_sem=sg_sem.at[h],
                recv_sem=rg_sem.at[h],
                device_id={"head": (my_head + step) % nhead},
                device_id_type=MESH,
            ).start()

    def await_heads(sem, h):
        if nhead == 1:
            return
        part = gath.at[h, pl.ds(0, nhead - 1)]
        pltpu.make_async_copy(part, part, sem.at[h]).wait()

    def project(h):
        left = jnp.concatenate([gath[h, y] for y in range(nhead)], axis=1)
        right = jnp.concatenate([w_ref[(y * per + h) * HD : (y * per + h + 1) * HD] for y in range(nhead)], axis=0)
        return dot(left, right)

    def give_back(h):
        await_rows(recv_x, rx_sem, h)
        attend(h)
        push(send_o, recv_o, so_sem, ro_sem, h)
        push(send_l, recv_l, sl_sem, rl_sem, h)

    def settle(h):
        await_all(recv_o, ro_sem, h)
        await_all(recv_l, rl_sem, h)
        mix(h)
        push_heads(h)

    find_seats()
    for h in range(per):
        await_shard(h, 0)
    pl.semaphore_wait(barrier, nseq + nhead - 2)
    ring_seats(0)
    ring_shards(0, 0)
    ring_shards(1, 0)
    near(0, (0,))
    for j in (1, 2):
        await_seats(j)
        await_shard(0, j)
    ring_seats(1)
    ring_shards(0, 1)
    ring_shards(2, 0)
    near(0, (1, 2))
    near(1, (0,))
    for j in (1, 2):
        await_shard(1, j)
    ring_shards(1, 1)
    near(1, (1, 2))
    for j in (3, 4):
        await_seats(j)
        await_shard(0, j)
    relay(0)
    near(2, (0,))
    for j in (1, 2):
        await_shard(2, j)
    ring_shards(2, 1)
    near(2, (1, 2))
    for j in (3, 4):
        await_shard(1, j)
    relay(1)
    give_back(0)
    for j in (3, 4):
        await_shard(2, j)
    relay(2)
    give_back(1)
    settle(0)
    give_back(2)
    settle(1)
    w_copy.wait()
    await_heads(rg_sem, 0)
    total = project(0)
    settle(2)
    await_heads(rg_sem, 1)
    total = total + project(1)
    await_heads(rg_sem, 2)
    out_ref[...] = (total + project(2)).astype(BF16)
    part = seats.at[pl.ds(0, 4)]
    pltpu.make_async_copy(part, part, seat_send).wait()
    for h in range(per):
        part = shard.at[h, pl.ds(0, 4)]
        pltpu.make_async_copy(part, part, ring_send.at[h]).wait()
        await_rows(recv_x, sx_sem, h)
        await_all(send_o, so_sem, h)
        await_all(send_l, sl_sem, h)
        await_heads(sg_sem, h)


def solution(mesh):
    nseq, nhead = mesh.shape["seq"], mesh.shape["head"]

    def body(q_in, k_in, v_in, q_rank, k_rank, w_out):
        length, width = q_in.shape
        rounds, per, _ = q_rank.shape
        cap = 2 * length // nseq
        vmem = pl.BlockSpec(memory_space=pltpu.VMEM)
        hbm = pl.BlockSpec(memory_space=pltpu.HBM)
        inner = nseq // PLANES
        scratch = [
            pltpu.VMEM(w_out.shape, BF16),
            pltpu.VMEM((per, 5, 3, length, HD), BF16),
            pltpu.VMEM((5, -(-2 * rounds * per // 8) * 8, length), F32),
            pltpu.VMEM((per, 9, inner, 3, rounds * cap, HD), BF16),
            pltpu.VMEM((per, nseq, 3, rounds * cap, HD), BF16),
            pltpu.VMEM((per, nseq, rounds * cap, HD), BF16),
            pltpu.VMEM((per, nseq, rounds * cap, HD), BF16),
            pltpu.VMEM((per, nseq, 1, HD), F32),
            pltpu.VMEM((per, nseq, 1, HD), F32),
            pltpu.VMEM((per, nhead, length, HD), BF16),
            pltpu.VMEM((rounds, per, nseq, length), F32),
            pltpu.VMEM((rounds, per, 1, length), F32),
            pltpu.SemaphoreType.DMA,
            pltpu.SemaphoreType.DMA,
            pltpu.SemaphoreType.DMA((5,)),
            pltpu.SemaphoreType.DMA((per,)),
            pltpu.SemaphoreType.DMA((per, 5)),
        ] + [pltpu.SemaphoreType.DMA((per,))] * 8
        return pl.pallas_call(
            functools.partial(kernel, (nseq, nhead, per, rounds, length)),
            out_shape=jax.ShapeDtypeStruct((length, w_out.shape[1]), BF16),
            in_specs=[hbm] * 3 + [vmem] * 2 + [hbm],
            out_specs=vmem,
            scratch_shapes=scratch,
            compiler_params=pltpu.CompilerParams(
                collective_id=0, has_side_effects=True, vmem_limit_bytes=48 * 1024 * 1024
            ),
        )(q_in, k_in, v_in, q_rank, k_rank, w_out)

    return jax.shard_map(
        body,
        mesh=mesh,
        in_specs=(
            P("seq", "head"),
            P("seq", "head"),
            P("seq", "head"),
            P(None, "head", "seq"),
            P(None, "head", "seq"),
            P(None, "head"),
        ),
        out_specs=P("seq", "head"),
        check_vma=False,
    )
```

```python
import functools

import jax
import jax.numpy as jnp
from jax import lax
from jax.experimental import pallas as pl
from jax.experimental.pallas import tpu as pltpu
from jax.sharding import PartitionSpec as P

MESH = pl.DeviceIdType.MESH
HD = 128
VMEM_BYTES = 63 * 1024 * 1024
PLANES = 8
EMPTY = 64.0
F32 = jnp.float32
BF16 = jnp.bfloat16


def dot(a, b, dims=((1,), (0,)), precision=None):
    return lax.dot_general(a, b, (dims, ((), ())), preferred_element_type=F32, precision=precision)


def kernel(
    sizes, q_hbm, k_hbm, v_hbm, qrank_hbm, krank_hbm, w_hbm, out_ref,
    qrank_ref, krank_ref, w_ref, shard, seats, packed, recv_x, send_o, recv_o, send_l, recv_l, gath, tq_ref, oq_ref,
    rank_sem, w_sem, seat_send, seat_recv, ring_send, ring_recv,
    sx_sem, rx_sem, so_sem, ro_sem, sl_sem, rl_sem, sg_sem, rg_sem, rf_sem,
):
    nseq, nhead, per, rounds, length = sizes
    cap = 2 * length // nseq
    slots = nseq * cap
    inner = nseq // PLANES
    me = lax.axis_index("seq")
    my_head = lax.axis_index("head")
    my_plane, my_place = me // inner, me % inner
    barrier = pltpu.get_barrier_semaphore()

    def plane_at(hop):
        return (my_plane + hop + PLANES) % PLANES

    def peer_of(step):
        return plane_at(step % PLANES) * inner + (my_place + step // PLANES) % inner

    @pl.loop(1, nseq)
    def _(step):
        pl.semaphore_signal(barrier, inc=1, device_id={"seq": peer_of(step)}, device_id_type=MESH)

    @pl.loop(1, nhead)
    def _(step):
        pl.semaphore_signal(barrier, inc=1, device_id={"head": (my_head + step) % nhead}, device_id_type=MESH)

    rank_copies = [
        pltpu.make_async_copy(qrank_hbm, qrank_ref, rank_sem.at[0]),
        pltpu.make_async_copy(krank_hbm, krank_ref, rank_sem.at[1]),
    ]
    for h in range(per):
        if h == 1:
            for copy in rank_copies:
                copy.start()
        for i, source in enumerate((q_hbm, k_hbm, v_hbm)):
            pltpu.make_async_copy(source.at[:, pl.ds(h * HD, HD)], shard.at[h, 0, i], ring_recv.at[h, 0]).start()
    w_copy = pltpu.make_async_copy(w_hbm, w_ref, w_sem)
    w_copy.start()

    def find_seats():
        shard_ids = lax.broadcasted_iota(jnp.int32, (nseq, length), 0)
        earlier = (
            lax.broadcasted_iota(jnp.int32, (length, length), 0)
            < lax.broadcasted_iota(jnp.int32, (length, length), 1)
        ).astype(F32).astype(BF16)
        seats[0] = jnp.zeros(seats.shape[1:], F32)
        for side, rank_ref in enumerate((qrank_ref, krank_ref)):
            for r in range(rounds):
                for h in range(per):
                    target = rank_ref[h, r : r + 1, :] // length
                    owner = (target == shard_ids).astype(F32)
                    before = dot(owner.astype(BF16), earlier)
                    ordinal = jnp.sum(owner * before, axis=0, keepdims=True)
                    row = (side * rounds + r) * per + h
                    seats[0, row : row + 1] = (target * cap).astype(F32) + ordinal
                    if side == 0:
                        tq_ref[r, h] = owner
                        oq_ref[r, h] = ordinal

    def seat_row(j, side, r, h):
        row = (side * rounds + r) * per + h
        return seats[j, row : row + 1].astype(jnp.int32)

    def ring(buf, h, send_sem, recv_sem, source, target, hop):
        at = (lambda j: buf.at[j]) if h is None else (lambda j: buf.at[h, j])
        pltpu.make_async_remote_copy(
            src_ref=at(source),
            dst_ref=at(target),
            send_sem=send_sem,
            recv_sem=recv_sem.at[target] if h is None else recv_sem.at[h, target],
            device_id={"seq": plane_at(hop) * inner + my_place},
            device_id_type=MESH,
        ).start()

    def ring_shards(h, stage):
        for (source, target), hop in zip(((0, 1), (0, 2)) if stage == 0 else ((1, 3), (2, 4)), (1, -1)):
            ring(shard, h, ring_send.at[h], ring_recv, source, target, hop)

    def ring_seats(stage):
        for (source, target), hop in zip(((0, 1), (0, 2)) if stage == 0 else ((1, 3), (2, 4)), (1, -1)):
            ring(seats, None, seat_send, seat_recv, source, target, hop)

    def await_shard(h, j):
        pltpu.make_async_copy(shard.at[h, j], shard.at[h, j], ring_recv.at[h, j]).wait()

    def await_seats(j):
        pltpu.make_async_copy(seats.at[j], seats.at[j], seat_recv.at[j]).wait()

    def pack(h, j, targets):
        n = len(targets) * inner
        ids = [lax.broadcasted_iota(jnp.int32, (inner * cap, length), 0) + plane * (inner * cap) for plane, _ in targets]
        ids = jnp.concatenate(ids, axis=0)
        q_all = shard[h, j, 0]
        kv_all = jnp.concatenate([shard[h, j, 1], shard[h, j, 2]], axis=1)
        q_rows, k_rows, v_rows = [], [], []
        for r in range(rounds):
            place = (ids == seat_row(j, 0, r, h)).astype(F32).astype(BF16)
            q_rows.append(dot(place, q_all).reshape(n, cap, HD))
            place = (ids == seat_row(j, 1, r, h)).astype(F32)
            filled = jnp.sum(place, axis=1, keepdims=True) > 0.5
            both = dot(place.astype(BF16), kv_all)
            k_rows.append(jnp.where(filled, both[:, :HD], EMPTY).reshape(n, cap, HD))
            v_rows.append(both[:, HD:].reshape(n, cap, HD))
        for i, rows in enumerate((q_rows, k_rows, v_rows)):
            rows = jnp.concatenate(rows, axis=1).astype(BF16)
            for t, (_, index) in enumerate(targets):
                packed[h, index, :, i] = rows[t * inner : (t + 1) * inner]

    def deliver(h, index, place, plane, source):
        pltpu.make_async_remote_copy(
            src_ref=packed.at[h, index, place],
            dst_ref=recv_x.at[h, source],
            send_sem=sx_sem.at[h],
            recv_sem=rx_sem.at[h],
            device_id={"seq": plane * inner + place},
            device_id_type=MESH,
        ).start()

    def near(h, js):
        for j in js:
            source = plane_at((0, -1, 1, -2, 2)[j]) * inner + my_place
            pack(h, j, [(my_plane, j)])
            recv_x[h, source] = packed[h, j, my_place]

            @pl.loop(1, inner)
            def _(step):
                deliver(h, j, (my_place + step) % inner, my_plane, source)

    def relay(h):
        for j, way in ((3, 1), (4, -1)):
            source = plane_at(-2 * way) * inner + my_place
            one, two = 2 * j - 1, 2 * j
            pack(h, j, [(my_plane, j), (plane_at(way), one), (plane_at(2 * way), two)])

            @pl.loop(0, inner)
            def _(step):
                deliver(h, one, (my_place + step) % inner, plane_at(way), source)

            odd = j - 3
            half = (inner + 1 - odd) // 2

            @pl.loop(0, half)
            def _(step):
                deliver(h, two, 2 * ((my_place // 2 + step) % half) + odd, plane_at(2 * way), source)

            recv_x[h, source] = packed[h, j, my_place]

            @pl.loop(1, inner)
            def _(step):
                deliver(h, j, (my_place + step) % inner, my_plane, source)

    def await_rows(buf, sem, h):
        part = recv_x.at[h, pl.ds(0, nseq - 5)]
        pltpu.make_async_copy(part, part, sem.at[h]).wait()

    def by_peer(rows):
        return rows.reshape(nseq, cap, HD)

    def push(send, recv, send_sem, recv_sem, h):
        recv[h, me] = send[h, me]

        @pl.loop(1, nseq)
        def _(step):
            peer = peer_of(step)
            pltpu.make_async_remote_copy(
                src_ref=send.at[h, peer],
                dst_ref=recv.at[h, me],
                send_sem=send_sem.at[h],
                recv_sem=recv_sem.at[h],
                device_id={"seq": peer},
                device_id_type=MESH,
            ).start()

    def await_all(buf, sem, h):
        part = buf.at[h, pl.ds(0, nseq - 1)]
        pltpu.make_async_copy(part, part, sem.at[h]).wait()

    def attend(h):
        lane = lax.broadcasted_iota(jnp.int32, (slots, HD), 1)
        row = lax.broadcasted_iota(jnp.int32, (slots, HD), 0)
        column_shard = lax.broadcasted_iota(jnp.int32, (nseq, slots), 1) // cap
        same_shard = column_shard == lax.broadcasted_iota(jnp.int32, (nseq, slots), 0)
        block = slots // 2
        out_rows = []
        logs = jnp.zeros((nseq, HD), F32)
        for r in range(rounds):

            def half(i):
                tile = recv_x[h, :, i].astype(F32)
                return tile[:, r * cap : (r + 1) * cap].reshape(slots, HD)

            q_all = half(0).astype(BF16)
            k_all = half(1)
            empty = k_all > 0.5 * EMPTY
            k_all = k_all.astype(BF16)
            v_all = half(2).astype(BF16)
            empty = jnp.concatenate([empty.astype(F32)] * (block // HD), axis=1) > 0.5 if block > HD else empty[:, :block]
            parts, log_parts = [], []
            for c in range(2):
                scores = dot(k_all, q_all[c * block : (c + 1) * block], ((1,), (1,))) * HD ** (-0.5)
                scores = jnp.where(empty, -1e30, scores)
                peak = jnp.max(scores, axis=0, keepdims=True)
                weights = jnp.exp(scores - peak)
                total = jnp.sum(weights, axis=0, keepdims=True)
                weights = (weights * (1.0 / total)).astype(BF16)
                parts.append(dot(v_all, weights, ((0,), (0,))).T)
                log_parts.append(peak + jnp.log(total))
            out_rows.append(by_peer(jnp.concatenate(parts, axis=0)))
            log_row = jnp.concatenate(log_parts, axis=1)
            spread = jnp.where(same_shard, log_row, 0.0)
            seat = (lane == row % cap + r * cap).astype(F32)
            logs = logs + dot(spread, seat, precision=lax.Precision.HIGHEST)
        send_o[h] = jnp.concatenate(out_rows, axis=1).astype(BF16)
        for d in range(nseq):
            send_l[h, d] = logs[d : d + 1]

    def mix(h):
        logs_in = jnp.concatenate([recv_l[h, d] for d in range(nseq)], axis=0)
        seat = lax.broadcasted_iota(jnp.int32, (cap, length), 0).astype(F32)
        logs, rows = [], []
        tile = recv_o[h].astype(F32)
        slot_ids = lax.broadcasted_iota(jnp.int32, (slots, length), 0)
        for r in range(rounds):
            of_owner = dot(logs_in, tq_ref[r, h], ((0,), (0,)), precision=lax.Precision.HIGHEST)
            mine = jnp.where(seat == oq_ref[r, h], of_owner[r * cap : (r + 1) * cap], 0.0)
            logs.append(jnp.sum(mine, axis=0, keepdims=True))
            part = tile[:, r * cap : (r + 1) * cap].reshape(slots, HD).astype(BF16)
            place = (slot_ids == seat_row(0, 0, r, h)).astype(F32).astype(BF16)
            rows.append(dot(part, place, ((0,), (0,))))
        peak = functools.reduce(jnp.maximum, logs)
        shares = [jnp.exp(log - peak) for log in logs]
        total = functools.reduce(jnp.add, shares)
        mixed = functools.reduce(jnp.add, [share / total * row for share, row in zip(shares, rows)])
        gath[h, my_head] = mixed.T.astype(BF16)

    def to_head(h, owner, hop, recv_sem, rows=None):
        part = gath.at[h, owner] if rows is None else gath.at[h, owner, rows]
        pltpu.make_async_remote_copy(
            src_ref=part,
            dst_ref=part,
            send_sem=sg_sem.at[h],
            recv_sem=recv_sem,
            device_id={"head": (my_head + hop + nhead) % nhead},
            device_id_type=MESH,
        ).start()

    def push_heads(h):
        if nhead != 8:
            for hop in range(1, nhead):
                to_head(h, my_head, hop, rg_sem.at[h])
            return
        for i, way in enumerate((1, -1)):
            to_head(h, my_head, 2 * way, rf_sem.at[h, i])
        for way in (1, -1):
            to_head(h, my_head, way, rg_sem.at[h])

    def relay_heads(h):
        if nhead != 8:
            return
        for i, way in enumerate((1, -1)):
            owner = (my_head - 2 * way + nhead) % nhead
            pltpu.make_async_copy(gath.at[h, owner], gath.at[h, owner], rf_sem.at[h, i]).wait()
            to_head(h, owner, way, rg_sem.at[h])
            to_head(h, owner, 2 * way, rg_sem.at[h], pl.ds(i * (length // 2), length // 2))

    def await_heads(sem, h):
        count = nhead - 1 if sem is sg_sem or nhead != 8 else nhead - 3
        if count:
            part = gath.at[h, pl.ds(0, count)]
            pltpu.make_async_copy(part, part, sem.at[h]).wait()

    def project(h):
        left = jnp.concatenate([gath[h, y] for y in range(nhead)], axis=1)
        right = jnp.concatenate([w_ref[(y * per + h) * HD : (y * per + h + 1) * HD] for y in range(nhead)], axis=0)
        return dot(left, right)

    def give_back(h):
        await_rows(recv_x, rx_sem, h)
        attend(h)
        push(send_o, recv_o, so_sem, ro_sem, h)
        push(send_l, recv_l, sl_sem, rl_sem, h)

    def settle(h):
        await_all(recv_o, ro_sem, h)
        await_all(recv_l, rl_sem, h)
        mix(h)
        push_heads(h)

    await_shard(0, 0)
    pl.semaphore_wait(barrier, nseq + nhead - 2)
    ring_shards(0, 0)
    await_shard(1, 0)
    ring_shards(1, 0)
    for copy in rank_copies:
        copy.wait()
    find_seats()
    ring_seats(0)
    await_shard(2, 0)
    near(0, (0,))
    for j in (1, 2):
        await_seats(j)
        await_shard(0, j)
    ring_seats(1)
    ring_shards(0, 1)
    ring_shards(2, 0)
    near(0, (1, 2))
    near(1, (0,))
    for j in (1, 2):
        await_shard(1, j)
    ring_shards(1, 1)
    near(1, (1, 2))
    for j in (3, 4):
        await_seats(j)
        await_shard(0, j)
    relay(0)
    near(2, (0,))
    for j in (1, 2):
        await_shard(2, j)
    ring_shards(2, 1)
    near(2, (1, 2))
    for j in (3, 4):
        await_shard(1, j)
    relay(1)
    give_back(0)
    for j in (3, 4):
        await_shard(2, j)
    relay(2)
    give_back(1)
    settle(0)
    relay_heads(0)
    give_back(2)
    settle(1)
    relay_heads(1)
    w_copy.wait()
    await_heads(rg_sem, 0)
    total = project(0)
    settle(2)
    relay_heads(2)
    await_heads(rg_sem, 1)
    total = total + project(1)
    await_heads(rg_sem, 2)
    out_ref[...] = (total + project(2)).astype(BF16)
    part = seats.at[pl.ds(0, 4)]
    pltpu.make_async_copy(part, part, seat_send).wait()
    for h in range(per):
        part = shard.at[h, pl.ds(0, 4)]
        pltpu.make_async_copy(part, part, ring_send.at[h]).wait()
        await_rows(recv_x, sx_sem, h)
        await_all(send_o, so_sem, h)
        await_all(send_l, sl_sem, h)
        await_heads(sg_sem, h)


def solution(mesh):
    nseq, nhead = mesh.shape["seq"], mesh.shape["head"]

    def body(q_in, k_in, v_in, q_rank, k_rank, w_out):
        length, width = q_in.shape
        rounds, per, _ = q_rank.shape
        cap = 2 * length // nseq
        vmem = pl.BlockSpec(memory_space=pltpu.VMEM)
        hbm = pl.BlockSpec(memory_space=pltpu.HBM)
        inner = nseq // PLANES
        scratch = [
            pltpu.VMEM((per, rounds, length), jnp.int32),
            pltpu.VMEM((per, rounds, length), jnp.int32),
            pltpu.VMEM(w_out.shape, BF16),
            pltpu.VMEM((per, 5, 3, length, HD), BF16),
            pltpu.VMEM((5, -(-2 * rounds * per // 8) * 8, length), F32),
            pltpu.VMEM((per, 9, inner, 3, rounds * cap, HD), BF16),
            pltpu.VMEM((per, nseq, 3, rounds * cap, HD), BF16),
            pltpu.VMEM((per, nseq, rounds * cap, HD), BF16),
            pltpu.VMEM((per, nseq, rounds * cap, HD), BF16),
            pltpu.VMEM((per, nseq, 1, HD), F32),
            pltpu.VMEM((per, nseq, 1, HD), F32),
            pltpu.VMEM((per, nhead, length, HD), BF16),
            pltpu.VMEM((rounds, per, nseq, length), F32),
            pltpu.VMEM((rounds, per, 1, length), F32),
            pltpu.SemaphoreType.DMA((2,)),
            pltpu.SemaphoreType.DMA,
            pltpu.SemaphoreType.DMA,
            pltpu.SemaphoreType.DMA((5,)),
            pltpu.SemaphoreType.DMA((per,)),
            pltpu.SemaphoreType.DMA((per, 5)),
        ] + [pltpu.SemaphoreType.DMA((per,))] * 8 + [pltpu.SemaphoreType.DMA((per, 2))]
        return pl.pallas_call(
            functools.partial(kernel, (nseq, nhead, per, rounds, length)),
            out_shape=jax.ShapeDtypeStruct((length, w_out.shape[1]), BF16),
            in_specs=[hbm] * 6,
            out_specs=vmem,
            scratch_shapes=scratch,
            compiler_params=pltpu.CompilerParams(
                collective_id=0, has_side_effects=True, vmem_limit_bytes=VMEM_BYTES
            ),
        )(q_in, k_in, v_in, jnp.transpose(q_rank, (1, 0, 2)), jnp.transpose(k_rank, (1, 0, 2)), w_out)

    return jax.shard_map(
        body,
        mesh=mesh,
        in_specs=(
            P("seq", "head"),
            P("seq", "head"),
            P("seq", "head"),
            P(None, "head", "seq"),
            P(None, "head", "seq"),
            P(None, "head"),
        ),
        out_specs=P("seq", "head"),
        check_vma=False,
    )
```

```python
import functools

import jax
import jax.numpy as jnp
from jax import lax
from jax.experimental import pallas as pl
from jax.experimental.pallas import tpu as pltpu
from jax.sharding import PartitionSpec as P

MESH = pl.DeviceIdType.MESH
HD = 128
VMEM_BYTES = 63 * 1024 * 1024
PLANES = 8
EMPTY = 64.0
F32 = jnp.float32
BF16 = jnp.bfloat16


def dot(a, b, dims=((1,), (0,)), precision=None):
    return lax.dot_general(a, b, (dims, ((), ())), preferred_element_type=F32, precision=precision)


def kernel(
    sizes, q_hbm, k_hbm, v_hbm, qrank_hbm, krank_hbm, w_hbm, out_ref,
    qrank_ref, krank_ref, w_ref, shard, seats, packed, recv_x, send_o, recv_o, send_l, recv_l, gath, tq_ref, oq_ref,
    rank_sem, w_sem, seat_send, seat_recv, ring_send, ring_recv,
    sx_sem, rx_sem, so_sem, ro_sem, sl_sem, rl_sem, sg_sem, rg_sem, rf_sem,
):
    nseq, nhead, per, rounds, length = sizes
    cap = 2 * length // nseq
    slots = nseq * cap
    inner = nseq // PLANES
    me = lax.axis_index("seq")
    my_head = lax.axis_index("head")
    my_plane, my_place = me // inner, me % inner
    barrier = pltpu.get_barrier_semaphore()

    def plane_at(hop):
        return (my_plane + hop + PLANES) % PLANES

    def peer_of(step):
        return plane_at(step % PLANES) * inner + (my_place + step // PLANES) % inner

    rank_copies = [
        pltpu.make_async_copy(qrank_hbm, qrank_ref, rank_sem.at[0]),
        pltpu.make_async_copy(krank_hbm, krank_ref, rank_sem.at[1]),
    ]
    for h in range(per):
        if h == 1:
            for copy in rank_copies:
                copy.start()
        for i, source in enumerate((q_hbm, k_hbm, v_hbm)):
            pltpu.make_async_copy(source.at[:, pl.ds(h * HD, HD)], shard.at[h, 0, i], ring_recv.at[h, 0]).start()
    @pl.loop(1, nseq)
    def _(step):
        pl.semaphore_signal(barrier, inc=1, device_id={"seq": peer_of(step)}, device_id_type=MESH)

    @pl.loop(1, nhead)
    def _(step):
        pl.semaphore_signal(barrier, inc=1, device_id={"head": (my_head + step) % nhead}, device_id_type=MESH)

    w_copy = pltpu.make_async_copy(w_hbm, w_ref, w_sem)
    w_copy.start()

    def find_seats():
        shard_ids = lax.broadcasted_iota(jnp.int32, (nseq, length), 0)
        earlier = (
            lax.broadcasted_iota(jnp.int32, (length, length), 0)
            < lax.broadcasted_iota(jnp.int32, (length, length), 1)
        ).astype(F32).astype(BF16)
        seats[0] = jnp.zeros(seats.shape[1:], F32)
        for side, rank_ref in enumerate((qrank_ref, krank_ref)):
            for r in range(rounds):
                for h in range(per):
                    target = rank_ref[h, r : r + 1, :] // length
                    owner = (target == shard_ids).astype(F32)
                    before = dot(owner.astype(BF16), earlier)
                    ordinal = jnp.sum(owner * before, axis=0, keepdims=True)
                    row = (side * rounds + r) * per + h
                    seats[0, row : row + 1] = (target * cap).astype(F32) + ordinal
                    if side == 0:
                        tq_ref[r, h] = owner
                        oq_ref[r, h] = ordinal

    def seat_row(j, side, r, h):
        row = (side * rounds + r) * per + h
        return seats[j, row : row + 1].astype(jnp.int32)

    def ring(buf, h, send_sem, recv_sem, source, target, hop):
        at = (lambda j: buf.at[j]) if h is None else (lambda j: buf.at[h, j])
        pltpu.make_async_remote_copy(
            src_ref=at(source),
            dst_ref=at(target),
            send_sem=send_sem,
            recv_sem=recv_sem.at[target] if h is None else recv_sem.at[h, target],
            device_id={"seq": plane_at(hop) * inner + my_place},
            device_id_type=MESH,
        ).start()

    def ring_shards(h, stage):
        for (source, target), hop in zip(((0, 1), (0, 2)) if stage == 0 else ((1, 3), (2, 4)), (1, -1)):
            ring(shard, h, ring_send.at[h], ring_recv, source, target, hop)

    def ring_seats(stage):
        for (source, target), hop in zip(((0, 1), (0, 2)) if stage == 0 else ((1, 3), (2, 4)), (1, -1)):
            ring(seats, None, seat_send, seat_recv, source, target, hop)

    def await_shard(h, j):
        pltpu.make_async_copy(shard.at[h, j], shard.at[h, j], ring_recv.at[h, j]).wait()

    def await_seats(j):
        pltpu.make_async_copy(seats.at[j], seats.at[j], seat_recv.at[j]).wait()

    def pack(h, j, targets):
        n = len(targets) * inner
        ids = [lax.broadcasted_iota(jnp.int32, (inner * cap, length), 0) + plane * (inner * cap) for plane, _ in targets]
        ids = jnp.concatenate(ids, axis=0)
        q_all = shard[h, j, 0]
        kv_all = jnp.concatenate([shard[h, j, 1], shard[h, j, 2]], axis=1)
        q_rows, k_rows, v_rows = [], [], []
        for r in range(rounds):
            place = (ids == seat_row(j, 0, r, h)).astype(F32).astype(BF16)
            q_rows.append(dot(place, q_all).reshape(n, cap, HD))
            place = (ids == seat_row(j, 1, r, h)).astype(F32)
            filled = jnp.sum(place, axis=1, keepdims=True) > 0.5
            both = dot(place.astype(BF16), kv_all)
            k_rows.append(jnp.where(filled, both[:, :HD], EMPTY).reshape(n, cap, HD))
            v_rows.append(both[:, HD:].reshape(n, cap, HD))
        for i, rows in enumerate((q_rows, k_rows, v_rows)):
            rows = jnp.concatenate(rows, axis=1).astype(BF16)
            for t, (_, index) in enumerate(targets):
                packed[h, index, :, i] = rows[t * inner : (t + 1) * inner]

    def deliver(h, index, place, plane, source):
        pltpu.make_async_remote_copy(
            src_ref=packed.at[h, index, place],
            dst_ref=recv_x.at[h, source],
            send_sem=sx_sem.at[h],
            recv_sem=rx_sem.at[h],
            device_id={"seq": plane * inner + place},
            device_id_type=MESH,
        ).start()

    def near(h, js):
        for j in js:
            source = plane_at((0, -1, 1, -2, 2)[j]) * inner + my_place
            pack(h, j, [(my_plane, j)])
            recv_x[h, source] = packed[h, j, my_place]

            @pl.loop(1, inner)
            def _(step):
                deliver(h, j, (my_place + step) % inner, my_plane, source)

    def relay(h):
        for j, way in ((3, 1), (4, -1)):
            source = plane_at(-2 * way) * inner + my_place
            one, two = 2 * j - 1, 2 * j
            pack(h, j, [(my_plane, j), (plane_at(way), one), (plane_at(2 * way), two)])

            @pl.loop(0, inner)
            def _(step):
                deliver(h, one, (my_place + step) % inner, plane_at(way), source)

            odd = j - 3
            half = (inner + 1 - odd) // 2

            @pl.loop(0, half)
            def _(step):
                deliver(h, two, 2 * ((my_place // 2 + step) % half) + odd, plane_at(2 * way), source)

            recv_x[h, source] = packed[h, j, my_place]

            @pl.loop(1, inner)
            def _(step):
                deliver(h, j, (my_place + step) % inner, my_plane, source)

    def await_rows(buf, sem, h):
        part = recv_x.at[h, pl.ds(0, nseq - 5)]
        pltpu.make_async_copy(part, part, sem.at[h]).wait()

    def by_peer(rows):
        return rows.reshape(nseq, cap, HD)

    def push_back(h):
        recv_o[h, me] = send_o[h, me]
        recv_l[h, me] = send_l[h, me]

        @pl.loop(1, nseq)
        def _(step):
            peer = (step - 1) + (step - 1 + nseq - me) // nseq
            for send, recv, send_sem, recv_sem in ((send_o, recv_o, so_sem, ro_sem), (send_l, recv_l, sl_sem, rl_sem)):
                pltpu.make_async_remote_copy(
                    src_ref=send.at[h, peer],
                    dst_ref=recv.at[h, me],
                    send_sem=send_sem.at[h],
                    recv_sem=recv_sem.at[h],
                    device_id={"seq": peer},
                    device_id_type=MESH,
                ).start()

    def await_all(buf, sem, h):
        part = buf.at[h, pl.ds(0, nseq - 1)]
        pltpu.make_async_copy(part, part, sem.at[h]).wait()

    def attend(h):
        lane = lax.broadcasted_iota(jnp.int32, (slots, HD), 1)
        row = lax.broadcasted_iota(jnp.int32, (slots, HD), 0)
        column_shard = lax.broadcasted_iota(jnp.int32, (nseq, slots), 1) // cap
        same_shard = column_shard == lax.broadcasted_iota(jnp.int32, (nseq, slots), 0)
        block = slots // 2
        out_rows = []
        logs = jnp.zeros((nseq, HD), F32)
        for r in range(rounds):

            def half(i):
                tile = recv_x[h, :, i].astype(F32)
                return tile[:, r * cap : (r + 1) * cap].reshape(slots, HD)

            q_all = half(0).astype(BF16)
            k_all = half(1)
            empty = k_all > 0.5 * EMPTY
            k_all = k_all.astype(BF16)
            v_all = half(2).astype(BF16)
            empty = jnp.concatenate([empty.astype(F32)] * (block // HD), axis=1) > 0.5 if block > HD else empty[:, :block]
            parts, log_parts = [], []
            for c in range(2):
                scores = dot(k_all, q_all[c * block : (c + 1) * block], ((1,), (1,))) * HD ** (-0.5)
                scores = jnp.where(empty, -1e30, scores)
                peak = jnp.max(scores, axis=0, keepdims=True)
                weights = jnp.exp(scores - peak)
                total = jnp.sum(weights, axis=0, keepdims=True)
                weights = (weights * (1.0 / total)).astype(BF16)
                parts.append(dot(v_all, weights, ((0,), (0,))).T)
                log_parts.append(peak + jnp.log(total))
            out_rows.append(by_peer(jnp.concatenate(parts, axis=0)))
            log_row = jnp.concatenate(log_parts, axis=1)
            spread = jnp.where(same_shard, log_row, 0.0)
            seat = (lane == row % cap + r * cap).astype(F32)
            logs = logs + dot(spread, seat, precision=lax.Precision.HIGHEST)
        send_o[h] = jnp.concatenate(out_rows, axis=1).astype(BF16)
        for d in range(nseq):
            send_l[h, d] = logs[d : d + 1]

    def mix(h):
        logs_in = jnp.concatenate([recv_l[h, d] for d in range(nseq)], axis=0)
        seat = lax.broadcasted_iota(jnp.int32, (cap, length), 0).astype(F32)
        logs, rows = [], []
        tile = recv_o[h].astype(F32)
        slot_ids = lax.broadcasted_iota(jnp.int32, (slots, length), 0)
        for r in range(rounds):
            of_owner = dot(logs_in, tq_ref[r, h], ((0,), (0,)), precision=lax.Precision.HIGHEST)
            mine = jnp.where(seat == oq_ref[r, h], of_owner[r * cap : (r + 1) * cap], 0.0)
            logs.append(jnp.sum(mine, axis=0, keepdims=True))
            part = tile[:, r * cap : (r + 1) * cap].reshape(slots, HD).astype(BF16)
            place = (slot_ids == seat_row(0, 0, r, h)).astype(F32).astype(BF16)
            rows.append(dot(part, place, ((0,), (0,))))
        peak = functools.reduce(jnp.maximum, logs)
        shares = [jnp.exp(log - peak) for log in logs]
        total = functools.reduce(jnp.add, shares)
        mixed = functools.reduce(jnp.add, [share / total * row for share, row in zip(shares, rows)])
        gath[h, my_head] = mixed.T.astype(BF16)

    def to_head(h, owner, hop, recv_sem, rows=None):
        part = gath.at[h, owner] if rows is None else gath.at[h, owner, rows]
        pltpu.make_async_remote_copy(
            src_ref=part,
            dst_ref=part,
            send_sem=sg_sem.at[h],
            recv_sem=recv_sem,
            device_id={"head": (my_head + hop + nhead) % nhead},
            device_id_type=MESH,
        ).start()

    def push_heads(h):
        if nhead != 8:
            for hop in range(1, nhead):
                to_head(h, my_head, hop, rg_sem.at[h])
            return
        for i, way in enumerate((1, -1)):
            to_head(h, my_head, 2 * way, rf_sem.at[h, i])
        for way in (1, -1):
            to_head(h, my_head, way, rg_sem.at[h])

    def relay_heads(h):
        if nhead != 8:
            return
        for i, way in enumerate((1, -1)):
            owner = (my_head - 2 * way + nhead) % nhead
            pltpu.make_async_copy(gath.at[h, owner], gath.at[h, owner], rf_sem.at[h, i]).wait()
            to_head(h, owner, way, rg_sem.at[h])
            to_head(h, owner, 2 * way, rg_sem.at[h], pl.ds(i * (length // 2), length // 2))

    def await_heads(sem, h):
        count = nhead - 1 if sem is sg_sem or nhead != 8 else nhead - 3
        if count:
            part = gath.at[h, pl.ds(0, count)]
            pltpu.make_async_copy(part, part, sem.at[h]).wait()

    def project(h):
        left = jnp.concatenate([gath[h, y] for y in range(nhead)], axis=1)
        right = jnp.concatenate([w_ref[(y * per + h) * HD : (y * per + h + 1) * HD] for y in range(nhead)], axis=0)
        return dot(left, right)

    def give_back(h):
        await_rows(recv_x, rx_sem, h)
        attend(h)
        push_back(h)

    def settle(h):
        await_all(recv_o, ro_sem, h)
        await_all(recv_l, rl_sem, h)
        mix(h)
        push_heads(h)

    await_shard(0, 0)
    pl.semaphore_wait(barrier, nseq + nhead - 2)
    ring_shards(0, 0)
    await_shard(1, 0)
    ring_shards(1, 0)
    for copy in rank_copies:
        copy.wait()
    find_seats()
    ring_seats(0)
    await_shard(2, 0)
    for j in (1, 2):
        await_seats(j)
        await_shard(0, j)
    ring_seats(1)
    ring_shards(0, 1)
    ring_shards(2, 0)
    near(0, (0, 1, 2))
    for j in (1, 2):
        await_shard(1, j)
    ring_shards(1, 1)
    near(1, (0, 1, 2))
    for j in (3, 4):
        await_seats(j)
        await_shard(0, j)
    relay(0)
    for j in (1, 2):
        await_shard(2, j)
    ring_shards(2, 1)
    near(2, (0, 1, 2))
    for j in (3, 4):
        await_shard(1, j)
    relay(1)
    give_back(0)
    for j in (3, 4):
        await_shard(2, j)
    relay(2)
    give_back(1)
    settle(0)
    relay_heads(0)
    give_back(2)
    settle(1)
    relay_heads(1)
    w_copy.wait()
    await_heads(rg_sem, 0)
    total = project(0)
    settle(2)
    relay_heads(2)
    await_heads(rg_sem, 1)
    total = total + project(1)
    await_heads(rg_sem, 2)
    out_ref[...] = (total + project(2)).astype(BF16)
    part = seats.at[pl.ds(0, 4)]
    pltpu.make_async_copy(part, part, seat_send).wait()
    for h in range(per):
        part = shard.at[h, pl.ds(0, 4)]
        pltpu.make_async_copy(part, part, ring_send.at[h]).wait()
        await_rows(recv_x, sx_sem, h)
        await_all(send_o, so_sem, h)
        await_all(send_l, sl_sem, h)
        await_heads(sg_sem, h)


def solution(mesh):
    nseq, nhead = mesh.shape["seq"], mesh.shape["head"]

    def body(q_in, k_in, v_in, q_rank, k_rank, w_out):
        length, width = q_in.shape
        rounds, per, _ = q_rank.shape
        cap = 2 * length // nseq
        vmem = pl.BlockSpec(memory_space=pltpu.VMEM)
        hbm = pl.BlockSpec(memory_space=pltpu.HBM)
        inner = nseq // PLANES
        scratch = [
            pltpu.VMEM((per, rounds, length), jnp.int32),
            pltpu.VMEM((per, rounds, length), jnp.int32),
            pltpu.VMEM(w_out.shape, BF16),
            pltpu.VMEM((per, 5, 3, length, HD), BF16),
            pltpu.VMEM((5, -(-2 * rounds * per // 8) * 8, length), F32),
            pltpu.VMEM((per, 9, inner, 3, rounds * cap, HD), BF16),
            pltpu.VMEM((per, nseq, 3, rounds * cap, HD), BF16),
            pltpu.VMEM((per, nseq, rounds * cap, HD), BF16),
            pltpu.VMEM((per, nseq, rounds * cap, HD), BF16),
            pltpu.VMEM((per, nseq, 1, HD), F32),
            pltpu.VMEM((per, nseq, 1, HD), F32),
            pltpu.VMEM((per, nhead, length, HD), BF16),
            pltpu.VMEM((rounds, per, nseq, length), F32),
            pltpu.VMEM((rounds, per, 1, length), F32),
            pltpu.SemaphoreType.DMA((2,)),
            pltpu.SemaphoreType.DMA,
            pltpu.SemaphoreType.DMA,
            pltpu.SemaphoreType.DMA((5,)),
            pltpu.SemaphoreType.DMA((per,)),
            pltpu.SemaphoreType.DMA((per, 5)),
        ] + [pltpu.SemaphoreType.DMA((per,))] * 8 + [pltpu.SemaphoreType.DMA((per, 2))]
        return pl.pallas_call(
            functools.partial(kernel, (nseq, nhead, per, rounds, length)),
            out_shape=jax.ShapeDtypeStruct((length, w_out.shape[1]), BF16),
            in_specs=[hbm] * 6,
            out_specs=vmem,
            scratch_shapes=scratch,
            compiler_params=pltpu.CompilerParams(
                collective_id=0, has_side_effects=True, vmem_limit_bytes=VMEM_BYTES
            ),
        )(q_in, k_in, v_in, jnp.transpose(q_rank, (1, 0, 2)), jnp.transpose(k_rank, (1, 0, 2)), w_out)

    return jax.shard_map(
        body,
        mesh=mesh,
        in_specs=(
            P("seq", "head"),
            P("seq", "head"),
            P("seq", "head"),
            P(None, "head", "seq"),
            P(None, "head", "seq"),
            P(None, "head"),
        ),
        out_specs=P("seq", "head"),
        check_vma=False,
    )
```

```python
import functools

import jax
import jax.numpy as jnp
from jax import lax
from jax.experimental import pallas as pl
from jax.experimental.pallas import tpu as pltpu
from jax.sharding import PartitionSpec as P

MESH = pl.DeviceIdType.MESH
HD = 128
VMEM_BYTES = 63 * 1024 * 1024
PLANES = 8
EMPTY = 64.0
F32 = jnp.float32
BF16 = jnp.bfloat16


def dot(a, b, dims=((1,), (0,)), precision=None):
    return lax.dot_general(a, b, (dims, ((), ())), preferred_element_type=F32, precision=precision)


def kernel(
    sizes, q_hbm, k_hbm, v_hbm, qrank_hbm, krank_hbm, w_hbm, out_ref,
    qrank_ref, krank_ref, w_ref, shard, seats, packed, recv_x, send_o, recv_o, send_l, recv_l, gath, tq_ref, oq_ref,
    rank_sem, w_sem, seat_send, seat_recv, ring_send, ring_recv,
    sx_sem, rx_sem, so_sem, ro_sem, sl_sem, rl_sem, sg_sem, rg_sem, rf_sem,
):
    nseq, nhead, per, rounds, length = sizes
    cap = 2 * length // nseq
    slots = nseq * cap
    inner = nseq // PLANES
    me = lax.axis_index("seq")
    my_head = lax.axis_index("head")
    my_plane, my_place = me // inner, me % inner
    barrier = pltpu.get_barrier_semaphore()

    def plane_at(hop):
        return (my_plane + hop + PLANES) % PLANES

    def peer_of(step):
        return plane_at(step % PLANES) * inner + (my_place + step // PLANES) % inner

    rank_copies = [
        pltpu.make_async_copy(qrank_hbm, qrank_ref, rank_sem.at[0]),
        pltpu.make_async_copy(krank_hbm, krank_ref, rank_sem.at[1]),
    ]
    for h in range(per):
        if h == 1:
            for copy in rank_copies:
                copy.start()
        for i, source in enumerate((q_hbm, k_hbm, v_hbm)):
            pltpu.make_async_copy(source.at[:, pl.ds(h * HD, HD)], shard.at[h, 0, i], ring_recv.at[h, 0]).start()
    @pl.loop(1, nseq)
    def _(step):
        pl.semaphore_signal(barrier, inc=1, device_id={"seq": peer_of(step)}, device_id_type=MESH)

    @pl.loop(1, nhead)
    def _(step):
        pl.semaphore_signal(barrier, inc=1, device_id={"head": (my_head + step) % nhead}, device_id_type=MESH)

    w_copy = pltpu.make_async_copy(w_hbm, w_ref, w_sem)
    w_copy.start()

    def find_seats():
        shard_ids = lax.broadcasted_iota(jnp.int32, (nseq, length), 0)
        earlier = (
            lax.broadcasted_iota(jnp.int32, (length, length), 0)
            < lax.broadcasted_iota(jnp.int32, (length, length), 1)
        ).astype(F32).astype(BF16)
        seats[0] = jnp.zeros(seats.shape[1:], F32)
        for side, rank_ref in enumerate((qrank_ref, krank_ref)):
            for r in range(rounds):
                for h in range(per):
                    target = rank_ref[h, r : r + 1, :] // length
                    owner = (target == shard_ids).astype(F32)
                    before = dot(owner.astype(BF16), earlier)
                    ordinal = jnp.sum(owner * before, axis=0, keepdims=True)
                    row = (side * rounds + r) * per + h
                    seats[0, row : row + 1] = (target * cap).astype(F32) + ordinal
                    if side == 0:
                        tq_ref[r, h] = owner
                        oq_ref[r, h] = ordinal

    def seat_row(j, side, r, h):
        row = (side * rounds + r) * per + h
        return seats[j, row : row + 1].astype(jnp.int32)

    def ring(buf, h, send_sem, recv_sem, source, target, hop):
        at = (lambda j: buf.at[j]) if h is None else (lambda j: buf.at[h, j])
        pltpu.make_async_remote_copy(
            src_ref=at(source),
            dst_ref=at(target),
            send_sem=send_sem,
            recv_sem=recv_sem.at[target] if h is None else recv_sem.at[h, target],
            device_id={"seq": plane_at(hop) * inner + my_place},
            device_id_type=MESH,
        ).start()

    def ring_shards(h, stage):
        for (source, target), hop in zip(((0, 1), (0, 2)) if stage == 0 else ((1, 3), (2, 4)), (1, -1)):
            ring(shard, h, ring_send.at[h], ring_recv, source, target, hop)

    def ring_seats(stage):
        for (source, target), hop in zip(((0, 1), (0, 2)) if stage == 0 else ((1, 3), (2, 4)), (1, -1)):
            ring(seats, None, seat_send, seat_recv, source, target, hop)

    def await_shard(h, j):
        pltpu.make_async_copy(shard.at[h, j], shard.at[h, j], ring_recv.at[h, j]).wait()

    def await_seats(j):
        pltpu.make_async_copy(seats.at[j], seats.at[j], seat_recv.at[j]).wait()

    def pack(h, j, targets):
        n = len(targets) * inner
        ids = [lax.broadcasted_iota(jnp.int32, (inner * cap, length), 0) + plane * (inner * cap) for plane, _ in targets]
        ids = jnp.concatenate(ids, axis=0)
        q_all = shard[h, j, 0]
        kv_all = jnp.concatenate([shard[h, j, 1], shard[h, j, 2]], axis=1)
        q_rows, k_rows, v_rows = [], [], []
        for r in range(rounds):
            place = (ids == seat_row(j, 0, r, h)).astype(F32).astype(BF16)
            q_rows.append(dot(place, q_all).reshape(n, cap, HD))
            place = (ids == seat_row(j, 1, r, h)).astype(F32)
            filled = jnp.sum(place, axis=1, keepdims=True) > 0.5
            both = dot(place.astype(BF16), kv_all)
            k_rows.append(jnp.where(filled, both[:, :HD], EMPTY).reshape(n, cap, HD))
            v_rows.append(both[:, HD:].reshape(n, cap, HD))
        for i, rows in enumerate((q_rows, k_rows, v_rows)):
            rows = jnp.concatenate(rows, axis=1).astype(BF16)
            for t, (_, index) in enumerate(targets):
                packed[h, index, :, i] = rows[t * inner : (t + 1) * inner]

    def deliver(h, index, place, plane, source):
        pltpu.make_async_remote_copy(
            src_ref=packed.at[h, index, place],
            dst_ref=recv_x.at[h, source],
            send_sem=sx_sem.at[h],
            recv_sem=rx_sem.at[h],
            device_id={"seq": plane * inner + place},
            device_id_type=MESH,
        ).start()

    def near(h, js):
        for j in js:
            source = plane_at((0, -1, 1, -2, 2)[j]) * inner + my_place
            pack(h, j, [(my_plane, j)])
            recv_x[h, source] = packed[h, j, my_place]

            @pl.loop(1, inner)
            def _(step):
                deliver(h, j, (my_place + step) % inner, my_plane, source)

    def relay(h):
        for j, way in ((3, 1), (4, -1)):
            source = plane_at(-2 * way) * inner + my_place
            one, two = 2 * j - 1, 2 * j
            pack(h, j, [(plane_at(way), one), (plane_at(2 * way), two)])

            @pl.loop(0, inner)
            def _(step):
                deliver(h, one, (my_place + step) % inner, plane_at(way), source)

            odd = j - 3
            half = (inner + 1 - odd) // 2

            @pl.loop(0, half)
            def _(step):
                deliver(h, two, 2 * ((my_place // 2 + step) % half) + odd, plane_at(2 * way), source)

        near(h, (3, 4))

    def await_rows(buf, sem, h):
        part = recv_x.at[h, pl.ds(0, nseq - 5)]
        pltpu.make_async_copy(part, part, sem.at[h]).wait()

    def by_peer(rows):
        return rows.reshape(nseq, cap, HD)

    def push_back(h):
        recv_o[h, me] = send_o[h, me]
        recv_l[h, me] = send_l[h, me]

        @pl.loop(1, nseq)
        def _(step):
            peer = (step - 1) + (step - 1 + nseq - me) // nseq
            for send, recv, send_sem, recv_sem in ((send_o, recv_o, so_sem, ro_sem), (send_l, recv_l, sl_sem, rl_sem)):
                pltpu.make_async_remote_copy(
                    src_ref=send.at[h, peer],
                    dst_ref=recv.at[h, me],
                    send_sem=send_sem.at[h],
                    recv_sem=recv_sem.at[h],
                    device_id={"seq": peer},
                    device_id_type=MESH,
                ).start()

    def await_all(buf, sem, h):
        part = buf.at[h, pl.ds(0, nseq - 1)]
        pltpu.make_async_copy(part, part, sem.at[h]).wait()

    def attend(h):
        lane = lax.broadcasted_iota(jnp.int32, (slots, HD), 1)
        row = lax.broadcasted_iota(jnp.int32, (slots, HD), 0)
        column_shard = lax.broadcasted_iota(jnp.int32, (nseq, slots), 1) // cap
        same_shard = column_shard == lax.broadcasted_iota(jnp.int32, (nseq, slots), 0)
        block = slots // 2
        out_rows = []
        logs = jnp.zeros((nseq, HD), F32)
        for r in range(rounds):

            def half(i):
                tile = recv_x[h, :, i].astype(F32)
                return tile[:, r * cap : (r + 1) * cap].reshape(slots, HD)

            q_all = half(0).astype(BF16)
            k_all = half(1)
            empty = k_all > 0.5 * EMPTY
            k_all = k_all.astype(BF16)
            v_all = half(2).astype(BF16)
            empty = jnp.concatenate([empty.astype(F32)] * (block // HD), axis=1) > 0.5 if block > HD else empty[:, :block]
            parts, log_parts = [], []
            for c in range(2):
                scores = dot(k_all, q_all[c * block : (c + 1) * block], ((1,), (1,))) * HD ** (-0.5)
                scores = jnp.where(empty, -1e30, scores)
                peak = jnp.max(scores, axis=0, keepdims=True)
                weights = jnp.exp(scores - peak)
                total = jnp.sum(weights, axis=0, keepdims=True)
                weights = (weights * (1.0 / total)).astype(BF16)
                parts.append(dot(v_all, weights, ((0,), (0,))).T)
                log_parts.append(peak + jnp.log(total))
            out_rows.append(by_peer(jnp.concatenate(parts, axis=0)))
            log_row = jnp.concatenate(log_parts, axis=1)
            spread = jnp.where(same_shard, log_row, 0.0)
            seat = (lane == row % cap + r * cap).astype(F32)
            logs = logs + dot(spread, seat, precision=lax.Precision.HIGHEST)
        send_o[h] = jnp.concatenate(out_rows, axis=1).astype(BF16)
        for d in range(nseq):
            send_l[h, d] = logs[d : d + 1]

    def mix(h):
        logs_in = jnp.concatenate([recv_l[h, d] for d in range(nseq)], axis=0)
        seat = lax.broadcasted_iota(jnp.int32, (cap, length), 0).astype(F32)
        logs, rows = [], []
        tile = recv_o[h].astype(F32)
        slot_ids = lax.broadcasted_iota(jnp.int32, (slots, length), 0)
        for r in range(rounds):
            of_owner = dot(logs_in, tq_ref[r, h], ((0,), (0,)), precision=lax.Precision.HIGHEST)
            mine = jnp.where(seat == oq_ref[r, h], of_owner[r * cap : (r + 1) * cap], 0.0)
            logs.append(jnp.sum(mine, axis=0, keepdims=True))
            part = tile[:, r * cap : (r + 1) * cap].reshape(slots, HD).astype(BF16)
            place = (slot_ids == seat_row(0, 0, r, h)).astype(F32).astype(BF16)
            rows.append(dot(part, place, ((0,), (0,))))
        peak = functools.reduce(jnp.maximum, logs)
        shares = [jnp.exp(log - peak) for log in logs]
        total = functools.reduce(jnp.add, shares)
        mixed = functools.reduce(jnp.add, [share / total * row for share, row in zip(shares, rows)])
        gath[h, my_head] = mixed.T.astype(BF16)

    def to_head(h, owner, hop, recv_sem, rows=None):
        part = gath.at[h, owner] if rows is None else gath.at[h, owner, rows]
        pltpu.make_async_remote_copy(
            src_ref=part,
            dst_ref=part,
            send_sem=sg_sem.at[h],
            recv_sem=recv_sem,
            device_id={"head": (my_head + hop + nhead) % nhead},
            device_id_type=MESH,
        ).start()

    def push_heads(h):
        if nhead != 8:
            for hop in range(1, nhead):
                to_head(h, my_head, hop, rg_sem.at[h])
            return
        for i, way in enumerate((1, -1)):
            to_head(h, my_head, 2 * way, rf_sem.at[h, i])
        for way in (1, -1):
            to_head(h, my_head, way, rg_sem.at[h])

    def relay_heads(h):
        if nhead != 8:
            return
        for i, way in enumerate((1, -1)):
            owner = (my_head - 2 * way + nhead) % nhead
            pltpu.make_async_copy(gath.at[h, owner], gath.at[h, owner], rf_sem.at[h, i]).wait()
            to_head(h, owner, way, rg_sem.at[h])
            to_head(h, owner, 2 * way, rg_sem.at[h], pl.ds(i * (length // 2), length // 2))

    def await_heads(sem, h):
        count = nhead - 1 if sem is sg_sem or nhead != 8 else nhead - 3
        if count:
            part = gath.at[h, pl.ds(0, count)]
            pltpu.make_async_copy(part, part, sem.at[h]).wait()

    def project(h):
        left = jnp.concatenate([gath[h, y] for y in range(nhead)], axis=1)
        right = jnp.concatenate([w_ref[(y * per + h) * HD : (y * per + h + 1) * HD] for y in range(nhead)], axis=0)
        return dot(left, right)

    def project_owners(h, hops):
        owners = [(my_head + hop + nhead) % nhead for hop in hops]
        left = jnp.concatenate([gath[h, owner] for owner in owners], axis=1)
        starts = [pl.multiple_of((owner * per + h) * HD, HD) for owner in owners]
        return dot(left, jnp.concatenate([w_ref[pl.ds(start, HD)] for start in starts], axis=0))

    def give_back(h):
        await_rows(recv_x, rx_sem, h)
        attend(h)
        push_back(h)

    def settle(h):
        await_all(recv_o, ro_sem, h)
        await_all(recv_l, rl_sem, h)
        mix(h)
        push_heads(h)

    await_shard(0, 0)
    pl.semaphore_wait(barrier, nseq + nhead - 2)
    ring_shards(0, 0)
    await_shard(1, 0)
    ring_shards(1, 0)
    for copy in rank_copies:
        copy.wait()
    find_seats()
    ring_seats(0)
    await_shard(2, 0)
    for j in (1, 2):
        await_seats(j)
        await_shard(0, j)
    ring_seats(1)
    ring_shards(0, 1)
    ring_shards(2, 0)
    near(0, (0, 1, 2))
    for j in (1, 2):
        await_shard(1, j)
    ring_shards(1, 1)
    near(1, (0, 1, 2))
    for j in (3, 4):
        await_seats(j)
        await_shard(0, j)
    relay(0)
    for j in (1, 2):
        await_shard(2, j)
    ring_shards(2, 1)
    near(2, (0, 1, 2))
    for j in (3, 4):
        await_shard(1, j)
    relay(1)
    give_back(0)
    for j in (3, 4):
        await_shard(2, j)
    relay(2)
    give_back(1)
    settle(0)
    relay_heads(0)
    give_back(2)
    settle(1)
    relay_heads(1)
    w_copy.wait()
    await_heads(rg_sem, 0)
    total = project(0)
    settle(2)
    relay_heads(2)
    await_heads(rg_sem, 1)
    total = total + project(1)
    if nhead == 8:
        total = total + project_owners(2, (0, 2, -2))
        await_heads(rg_sem, 2)
        total = total + project_owners(2, (1, -1, 3, -3, 4))
    else:
        await_heads(rg_sem, 2)
        total = total + project(2)
    out_ref[...] = total.astype(BF16)
    part = seats.at[pl.ds(0, 4)]
    pltpu.make_async_copy(part, part, seat_send).wait()
    for h in range(per):
        part = shard.at[h, pl.ds(0, 4)]
        pltpu.make_async_copy(part, part, ring_send.at[h]).wait()
        await_rows(recv_x, sx_sem, h)
        await_all(send_o, so_sem, h)
        await_all(send_l, sl_sem, h)
        await_heads(sg_sem, h)


def solution(mesh):
    nseq, nhead = mesh.shape["seq"], mesh.shape["head"]

    def body(q_in, k_in, v_in, q_rank, k_rank, w_out):
        length, width = q_in.shape
        rounds, per, _ = q_rank.shape
        cap = 2 * length // nseq
        vmem = pl.BlockSpec(memory_space=pltpu.VMEM)
        hbm = pl.BlockSpec(memory_space=pltpu.HBM)
        inner = nseq // PLANES
        scratch = [
            pltpu.VMEM((per, rounds, length), jnp.int32),
            pltpu.VMEM((per, rounds, length), jnp.int32),
            pltpu.VMEM(w_out.shape, BF16),
            pltpu.VMEM((per, 5, 3, length, HD), BF16),
            pltpu.VMEM((5, -(-2 * rounds * per // 8) * 8, length), F32),
            pltpu.VMEM((per, 9, inner, 3, rounds * cap, HD), BF16),
            pltpu.VMEM((per, nseq, 3, rounds * cap, HD), BF16),
            pltpu.VMEM((per, nseq, rounds * cap, HD), BF16),
            pltpu.VMEM((per, nseq, rounds * cap, HD), BF16),
            pltpu.VMEM((per, nseq, 1, HD), F32),
            pltpu.VMEM((per, nseq, 1, HD), F32),
            pltpu.VMEM((per, nhead, length, HD), BF16),
            pltpu.VMEM((rounds, per, nseq, length), F32),
            pltpu.VMEM((rounds, per, 1, length), F32),
            pltpu.SemaphoreType.DMA((2,)),
            pltpu.SemaphoreType.DMA,
            pltpu.SemaphoreType.DMA,
            pltpu.SemaphoreType.DMA((5,)),
            pltpu.SemaphoreType.DMA((per,)),
            pltpu.SemaphoreType.DMA((per, 5)),
        ] + [pltpu.SemaphoreType.DMA((per,))] * 8 + [pltpu.SemaphoreType.DMA((per, 2))]
        return pl.pallas_call(
            functools.partial(kernel, (nseq, nhead, per, rounds, length)),
            out_shape=jax.ShapeDtypeStruct((length, w_out.shape[1]), BF16),
            in_specs=[hbm] * 6,
            out_specs=vmem,
            scratch_shapes=scratch,
            compiler_params=pltpu.CompilerParams(
                collective_id=0, has_side_effects=True, vmem_limit_bytes=VMEM_BYTES
            ),
        )(q_in, k_in, v_in, jnp.transpose(q_rank, (1, 0, 2)), jnp.transpose(k_rank, (1, 0, 2)), w_out)

    return jax.shard_map(
        body,
        mesh=mesh,
        in_specs=(
            P("seq", "head"),
            P("seq", "head"),
            P("seq", "head"),
            P(None, "head", "seq"),
            P(None, "head", "seq"),
            P(None, "head"),
        ),
        out_specs=P("seq", "head"),
        check_vma=False,
    )
```
